512 devices in a mesh: tm: 32 (over z, core), state: 16 (over y, x).
Axes of the slice: x: 4, y: 4, z: 16, core: 2. Of those that a mesh axis runs over, the one named last changes fastest.
Arguments:
- transition: float32 [1024, 1024], replicated, may hold values from -0.1 to 1.1
- prior_cov: float32 [1024, 1024], replicated, may hold values from -0.1 to 3.5, as said below
- noise_var: float32 [1024], replicated, may hold values from 0.2 to 30
- sensor_mask: int32 [32, 1024], P('tm'), may hold values 0 or 1
- readings: float32 [32, 1024], P('tm'), may hold values from -6 to 6
- prior_mean: float32 [1024], replicated, may hold values from -6 to 6
Outputs:
- filtered: float32 [32, 1024], P('tm', 'state')
The draws below stay inside these ranges and needn't reach their ends.
Inputs may be any that keep to these rules, and one draw needn't show every extreme that they name: `prior_cov`: symmetric and positive definite.
All inputs are finite; a program needn't handle non-finite values. Where the reference program divides by a largest or mean magnitude, that divisor is 1e-20 or more. No bound on the sum of `sensor_mask` on one device may be relied on, other than what follows from the above.
Results may differ from the reference program's by a relative error of at most 0.0003.
Values sent between devices are 32-bit elements; how exact they have to be, the bound alone decides.
A program may use at most 64 MiB of HBM per device.

```python
import math
import jax
import jax.numpy as jnp
from jax import lax

S = 1024
NS_STEPS = 8
BLOCKS = 32


def draw_transition(key, part):
    key = jax.random.fold_in(key, 11)
    diag_key, spread_key = jax.random.split(key)
    diagonal = jax.random.uniform(diag_key, (S,), jnp.float32, 0.95, 1.05)
    spread = jax.random.truncated_normal(spread_key, -3.0, 3.0, (S, S), jnp.float32) * 0.2
    return spread / S ** 0.5 + jnp.diag(diagonal)


def draw_prior_cov(key, part):
    key = jax.random.fold_in(key, 23)
    diag_key, spread_key = jax.random.split(key)
    diagonal = jax.random.uniform(diag_key, (S,), jnp.float32, 1.5, 3.0)
    raw = jax.random.truncated_normal(spread_key, -3.0, 3.0, (S, S), jnp.float32) * 0.5
    symmetric = (raw + raw.T) * 0.5 ** 0.5
    shared = 0.2 * jnp.ones((S, S), jnp.float32)
    return symmetric / S ** 0.5 + jnp.diag(diagonal) + shared


def plant(array, stream_key, least, high):
    place = [jax.random.randint(jax.random.fold_in(stream_key, axis), (), 0, length) for axis, length in enumerate(array.shape)]
    main_axis = array.shape.index(max(array.shape))
    neighbour = place[:main_axis] + [(place[main_axis] + 1) % array.shape[main_axis]] + place[main_axis + 1:]
    return array.at[tuple(place)].set(least).at[tuple(neighbour)].set(high)


def steps_of(own_key, shape, pieces, low, largest):
    gain = 1.0
    for axis_at, blocks in pieces:
        draws = jax.random.uniform(jax.random.fold_in(jax.random.fold_in(own_key, 6), axis_at), (blocks,), jnp.float32, low / len(pieces), largest / len(pieces))
        gain = gain * jnp.repeat(jnp.exp(draws), shape[axis_at] // blocks).reshape((-1,) + (1,) * (len(shape) - 1 - axis_at))
    return gain


def scatter_about(rng, shape, width, bound, shards=(), held_as=jnp.bfloat16):
    array = jax.random.normal(rng, shape, jnp.float32) * width
    if len(shards) > 0:
        array = steps_of(rng, shape, shards, -0.22, 0.18) * array
    return jnp.clip(array, min=-bound, max=bound).astype(held_as)


def setup_inputs(seed: int = 0) -> dict:
    arg_keys = jax.random.split(jax.random.key(seed), 7)
    return {
        "transition": draw_transition(jax.random.fold_in(arg_keys[6], 71), 0),
        "prior_cov": draw_prior_cov(jax.random.fold_in(arg_keys[6], 71), 0),
        "noise_var": jnp.clip(jnp.exp(jax.random.uniform(arg_keys[2], (S,), jnp.float32, math.log(0.2), math.log(30.0))), 0.2, 30.0),
        "sensor_mask": plant((jax.random.randint(arg_keys[3], (BLOCKS, S), 0, 4) < 3).astype(jnp.int32), jax.random.fold_in(arg_keys[3], 1), 0, 1),
        "readings": scatter_about(arg_keys[4], (BLOCKS, S), 1.0, 6.0, ((0, 32),), jnp.float32),
        "prior_mean": scatter_about(arg_keys[5], (S,), 1.0, 6.0, (), jnp.float32),
    }


HIGHEST = lax.Precision.HIGHEST


def matmul(former, latter):
    return jnp.dot(former, latter, precision=HIGHEST, preferred_element_type=jnp.float32)


def block_element(transition, prior_cov, noise_var, mask_row, reading_row):
    present = mask_row.astype(jnp.float32)
    system = present[:, None] * prior_cov * present[None, :] + jnp.diag(noise_var)
    scale_bound = jnp.max(jnp.sum(jnp.abs(system), axis=1))
    identity = jnp.eye(S, dtype=jnp.float32)
    iterate = 2.0 * identity / scale_bound - system / (scale_bound * scale_bound)
    for iteration in range(NS_STEPS - 1):
        iterate = 2.0 * iterate - matmul(matmul(iterate, system), iterate)
    weighted = prior_cov * present[None, :]
    step_map = transition - matmul(weighted, matmul(iterate, present[:, None] * transition))
    offset = matmul(weighted, matmul(iterate, present * reading_row))
    return step_map, offset


def reference(transition, prior_cov, noise_var, sensor_mask, readings, prior_mean):
    def element(inputs):
        return block_element(transition, prior_cov, noise_var, inputs[0], inputs[1])

    maps, offsets = lax.map(element, (sensor_mask, readings))

    def advance(running, element_pair):
        updated = matmul(element_pair[0], running) + element_pair[1]
        return updated, updated

    _, filtered = lax.scan(advance, prior_mean, (maps, offsets))
    return filtered
```

```python
import functools
import jax
import jax.numpy as jnp
from jax import lax
from jax.experimental import pallas as pl
from jax.experimental.pallas import tpu as pltpu
from jax.sharding import PartitionSpec as P

f32 = jnp.float32
bf16 = jnp.bfloat16
S = 1024
BLK = 256
LANE = 128
SQUARINGS = 7
T_SLOT, P_SLOT, Y_SLOT = 8, 9, 10
W_SLOT, M_SLOT, OTHER_SLOT = 0, 1, 7

PRODUCT_FROM = (1, 2, 2, 3, 3, 4, 5)
MAP_FROM = 8
SHIP_FROM = 9
MESH_ID = pl.DeviceIdType.MESH


def split(value):
    high = value.astype(bf16)
    return high, (value - high.astype(f32)).astype(bf16)


def dot(left, right):
    return jnp.dot(left, right, preferred_element_type=f32)


def dot3(left_high, left_low, right_high, right_low):
    return dot(left_high, right_high) + dot(left_high, right_low) + dot(left_low, right_high)


def matvec(mats, slot, x):
    parts = []
    for i in range(S // LANE):
        total = None
        for k in range(S // LANE):
            tile = mats[slot, pl.ds(i * LANE, LANE), pl.ds(k * LANE, LANE)]
            term = tile * x[:, k * LANE:(k + 1) * LANE]
            total = term if total is None else total + term
        parts.append(jnp.sum(total.T, axis=0, keepdims=True))
    return jnp.concatenate(parts, axis=1)


def mirror(mats, slot):
    for i in range(S // BLK):
        for j in range(i):
            rows, cols = pl.ds(i * BLK, BLK), pl.ds(j * BLK, BLK)
            mats[slot, rows, cols] = mats[slot, cols, rows].T


def split_into(mats, slot, high, low):
    for i in range(S // BLK):
        rows = pl.ds(i * BLK, BLK)
        high[rows, :], low[rows, :] = split(mats[slot, rows, :])


def upper_step(mats, source, target, lh, ll, rh, rl):
    for i in range(S // BLK):
        rows, cols = pl.ds(i * BLK, BLK), pl.ds(i * BLK, S - i * BLK)
        product = dot3(lh[rows, :], ll[rows, :], rh[:, cols], rl[:, cols])
        mats[target, rows, cols] = 2.0 * mats[source, rows, cols] - product
    mirror(mats, target)


def kernel(planes, t_hbm, p_hbm, noise_ref, mask_ref, read_ref, mean_ref, out_ref,
           mats, gh, gl, yh, yl, offset, other_offset, xin, xmid, xout, yvec, bound,
           load_sem, send_sem, recv_sem, ready_sem):
    tm = lax.axis_index("tm")
    state = lax.axis_index("state")
    z, core = lax.div(tm, 2), lax.rem(tm, 2)
    products = sum((z >= first).astype(jnp.int32) for first in PRODUCT_FROM)
    has_map = z >= MAP_FROM
    ships = z >= SHIP_FROM
    entry_core = ships.astype(jnp.int32)
    next_entry = (z + 1 >= SHIP_FROM).astype(jnp.int32)
    has_next = jnp.logical_and(core == 1, z < planes - 1)
    has_before = jnp.logical_and(core == entry_core, z > 0)

    barrier = pltpu.get_barrier_semaphore()

    def greet(where):
        pl.semaphore_signal(barrier, inc=1, device_id=(where, state), device_id_type=MESH_ID)

    partner = z * 2 + 1 - core
    following = (z + 1) * 2 + next_entry
    greet(partner)

    @pl.when(has_next)
    def _():
        greet(following)

    @pl.when(has_before)
    def _():
        greet((z - 1) * 2 + 1)

    load_p = pltpu.make_async_copy(p_hbm, mats.at[P_SLOT], load_sem.at[0])
    load_t = pltpu.make_async_copy(t_hbm, mats.at[T_SLOT], load_sem.at[1])
    load_p.start()
    load_t.start()

    present = mask_ref[...].astype(f32)
    observed = present * read_ref[...]
    row_id = lax.broadcasted_iota(jnp.int32, (LANE, LANE), 0)
    col_id = lax.broadcasted_iota(jnp.int32, (LANE, LANE), 1)
    on_diagonal = row_id == col_id

    load_p.wait()
    sums = [jnp.zeros((8, LANE), f32) for _ in range(S // LANE)]
    for i in range(S // LANE):
        rows = pl.ds(i * LANE, LANE)
        down = jnp.broadcast_to(present[:, i * LANE:(i + 1) * LANE], (LANE, LANE)).T
        for k in range(S // LANE):
            cols = pl.ds(k * LANE, LANE)
            tile = mats[P_SLOT, rows, cols] * present[:, k * LANE:(k + 1) * LANE] * down
            if i == k:
                tile = tile + jnp.where(on_diagonal, noise_ref[:, cols], 0.0)
            mats[0, rows, cols] = tile
            sums[k] = sums[k] + jnp.sum(jnp.abs(tile).reshape(LANE // 8, 8, LANE), axis=0)
    row_sums = jnp.concatenate([jnp.sum(part, axis=0, keepdims=True) for part in sums], axis=1)
    inverse_bound = 1.0 / jnp.max(row_sums, axis=1, keepdims=True)
    bound[...] = jnp.broadcast_to(inverse_bound, (1, LANE))
    for i in range(S // BLK):
        rows = pl.ds(i * BLK, BLK)
        scaled = mats[0, rows, :] * inverse_bound
        mats[0, rows, :] = scaled
        gh[rows, :], gl[rows, :] = split(scaled)

    def square(j, carry):
        upper_step(mats, j, j + 1, gh, gl, gh, gl)
        split_into(mats, j + 1, gh, gl)
        return carry

    lax.fori_loop(0, SQUARINGS, square, 0)

    @pl.when(products > 0)
    def _():
        scale = bound[:, :1]
        for i in range(S // LANE):
            rows = pl.ds(i * LANE, LANE)
            for k in range(S // LANE):
                cols = pl.ds(k * LANE, LANE)
                tile = -mats[0, rows, cols]
                if i == k:
                    tile = tile + jnp.where(on_diagonal, 2.0, 0.0)
                tile = tile * scale
                mats[Y_SLOT, rows, cols] = tile
                yh[rows, cols], yl[rows, cols] = split(tile)

    def multiply(q, carry):
        split_into(mats, q, gh, gl)
        upper_step(mats, Y_SLOT, Y_SLOT, yh, yl, gh, gl)
        split_into(mats, Y_SLOT, yh, yl)
        return carry

    lax.fori_loop(1, products + 1, multiply, 0)

    load_t.wait()

    @pl.when(has_map)
    def _():
        for i in range(S // BLK):
            rows = pl.ds(i * BLK, BLK)
            gh[rows, :], gl[rows, :] = split(mats[P_SLOT, rows, :] * present)
        for i in range(S // BLK):
            rows = pl.ds(i * BLK, BLK)
            mats[W_SLOT, rows, :] = dot3(gh[rows, :], gl[rows, :], yh[...], yl[...])
        offset[...] = matvec(mats, W_SLOT, observed)
        for i in range(S // BLK):
            rows = pl.ds(i * BLK, BLK)
            gh[rows, :], gl[rows, :] = split(mats[W_SLOT, rows, :] * present)
            yh[rows, :], yl[rows, :] = split(mats[T_SLOT, rows, :])
        for i in range(S // BLK):
            rows = pl.ds(i * BLK, BLK)
            mats[M_SLOT, rows, :] = mats[T_SLOT, rows, :] - dot3(gh[rows, :], gl[rows, :], yh[...], yl[...])

    pl.semaphore_wait(barrier, 1 + has_next.astype(jnp.int32) + has_before.astype(jnp.int32))

    def send(source, target, index, where):
        return pltpu.make_async_remote_copy(
            src_ref=source, dst_ref=target, send_sem=send_sem.at[index], recv_sem=recv_sem.at[index],
            device_id=(where, state), device_id_type=MESH_ID)

    mean_in = send(xout, xin, 0, following)
    map_over = send(mats.at[M_SLOT], mats.at[OTHER_SLOT], 1, partner)
    offset_over = send(offset, other_offset, 2, partner)

    @pl.when(jnp.logical_and(ships, core == 1))
    def _():
        pl.semaphore_signal(ready_sem, inc=1, device_id=(partner, state), device_id_type=MESH_ID)

    @pl.when(jnp.logical_and(ships, core == 0))
    def _():
        pl.semaphore_wait(ready_sem, 1)
        map_over.start()
        offset_over.start()

    @pl.when(jnp.logical_and(ships, core == 1))
    def _():
        map_over.wait_recv()
        offset_over.wait_recv()

    @pl.when(tm == 0)
    def _():
        xin[...] = mean_ref[...]

    @pl.when(tm > 0)
    def _():
        mean_in.wait_recv()

    middle_out = send(xmid, xin, 0, partner)

    @pl.when(jnp.logical_not(ships))
    def _():
        @pl.when(has_map)
        def _():
            xout[...] = matvec(mats, M_SLOT, xin[...]) + offset[...]

        @pl.when(jnp.logical_not(has_map))
        def _():
            moved = matvec(mats, T_SLOT, xin[...])
            gap = observed - present * moved

            @pl.when(products == 0)
            def _():
                yvec[...] = gap * bound[:, :1]

            @pl.when(products > 0)
            def _():
                yvec[...] = matvec(mats, Y_SLOT, gap)

            def apply(j, carry):
                y = yvec[...]
                yvec[...] = 2.0 * y - matvec(mats, j, y)
                return carry

            lax.fori_loop(jnp.where(products == 0, 0, products + 1), SQUARINGS + 1, apply, 0)
            xout[...] = moved + matvec(mats, P_SLOT, present * yvec[...])

    @pl.when(jnp.logical_and(ships, core == 1))
    def _():
        middle = matvec(mats, OTHER_SLOT, xin[...]) + other_offset[...]
        xmid[...] = middle
        middle_out.start()
        xout[...] = matvec(mats, M_SLOT, middle) + offset[...]

    @pl.when(jnp.logical_and(ships, core == 0))
    def _():
        xout[...] = xin[...]

    inner_out = send(xout, xin, 0, partner)
    inner = jnp.logical_and(jnp.logical_not(ships), core == 0)

    @pl.when(inner)
    def _():
        inner_out.start()

    @pl.when(has_next)
    def _():
        mean_in.start()

    out_ref[...] = xout[...]

    @pl.when(inner)
    def _():
        inner_out.wait_send()

    @pl.when(has_next)
    def _():
        mean_in.wait_send()

    @pl.when(jnp.logical_and(ships, core == 0))
    def _():
        map_over.wait_send()
        offset_over.wait_send()

    @pl.when(jnp.logical_and(ships, core == 1))
    def _():
        middle_out.wait_send()


def per_device(transition, prior_cov, noise_var, sensor_mask, readings, prior_mean):
    planes = lax.axis_size("tm") // 2
    row = lambda value: value.reshape(1, S)
    vmem = pl.BlockSpec(memory_space=pltpu.VMEM)
    hbm = pl.BlockSpec(memory_space=pl.ANY)
    vector = pltpu.VMEM((1, S), f32)
    half = pltpu.VMEM((S, S), bf16)
    mean = pl.pallas_call(
        functools.partial(kernel, planes),
        out_shape=jax.ShapeDtypeStruct((1, S), f32),
        in_specs=[hbm, hbm, vmem, vmem, vmem, vmem],
        out_specs=vmem,
        scratch_shapes=[
            pltpu.VMEM((11, S, S), f32), half, half, half, half,
            vector, vector, vector, vector, vector, vector, pltpu.VMEM((1, LANE), f32),
            pltpu.SemaphoreType.DMA((2,)), pltpu.SemaphoreType.DMA((3,)), pltpu.SemaphoreType.DMA((3,)),
            pltpu.SemaphoreType.REGULAR,
        ],
        compiler_params=pltpu.CompilerParams(
            collective_id=0, has_side_effects=True, vmem_limit_bytes=63 * 2 ** 20),
    )(transition, prior_cov, row(noise_var), sensor_mask, readings, row(prior_mean))
    share = S // lax.axis_size("state")
    return lax.dynamic_slice_in_dim(mean, lax.axis_index("state") * share, share, 1)


def solution(mesh):
    placed = (P(), P(), P(), P("tm", None), P("tm", None), P())
    return jax.shard_map(
        per_device, mesh=mesh, in_specs=placed, out_specs=P("tm", "state"), check_vma=False
    )
```

```python
import functools
import jax
import jax.numpy as jnp
from jax import lax
from jax.experimental import pallas as pl
from jax.experimental.pallas import tpu as pltpu
from jax.sharding import PartitionSpec as P

f32 = jnp.float32
bf16 = jnp.bfloat16
S = 1024
BLK = 256
LANE = 128
WIDE = 512
SQUARINGS = 7
FIRST_TOPS = (4, 5)
T_SLOT, P_SLOT = 8, 9
W_SLOT, M_SLOT, OTHER_SLOT = 0, 1, 7

PRODUCT_FROM = (2, 3, 3, 4, 4, 5, 5)
GAIN_FROM = 7
MAP_FROM = 9
SHIP_FROM = 9
MESH_ID = pl.DeviceIdType.MESH


def split(value):
    high = value.astype(bf16)
    return high, (value - high.astype(f32)).astype(bf16)


def dot(left, right):
    return jnp.dot(left, right, preferred_element_type=f32)


def dot3(left_high, left_low, right_high, right_low):
    return dot(left_high, right_high) + dot(left_high, right_low) + dot(left_low, right_high)


def matvec(mats, slot, x):
    parts = []
    for i in range(S // LANE):
        total = None
        for k in range(S // LANE):
            tile = mats[slot, pl.ds(i * LANE, LANE), pl.ds(k * LANE, LANE)]
            term = tile * x[:, k * LANE:(k + 1) * LANE]
            total = term if total is None else total + term
        parts.append(jnp.sum(total.T, axis=0, keepdims=True))
    return jnp.concatenate(parts, axis=1)


def column_parts(start, stop):
    return [pl.ds(at, min(WIDE, stop - at)) for at in range(start, stop, WIDE)]


def square(mats, source, target, gh, gl, now):
    later = 1 - now
    for i in range(S // BLK):
        rows = pl.ds(i * BLK, BLK)
        left = gh[now, rows, :]
        for j in range(i + 1, S // BLK):
            cols = pl.ds(j * BLK, BLK)
            mats[target, cols, rows] = dot(left, gl[now, :, cols]).T
        for cols in column_parts(0, i * BLK):
            product = dot(left, gh[now, :, cols]) + dot(left, gl[now, :, cols])
            new = 2.0 * mats[source, rows, cols] - product - mats[target, rows, cols]
            mats[target, rows, cols] = new
            gh[later, rows, cols], gl[later, rows, cols] = split(new)
        cross = dot(left, gl[now, :, rows])
        new = 2.0 * mats[source, rows, rows] - dot(left, gh[now, :, rows]) - (cross + cross.T)
        mats[target, rows, rows] = new
        gh[later, rows, rows], gl[later, rows, rows] = split(new)
        for j in range(i):
            cols = pl.ds(j * BLK, BLK)
            turned = mats[target, rows, cols].T
            mats[target, cols, rows] = turned
            gh[later, cols, rows], gl[later, cols, rows] = split(turned)


def multiply(whole, yh, yl, gh, gl, now):
    for i in range(S // BLK):
        rows = pl.ds(i * BLK, BLK)
        left_high, left_low = yh[rows, :], yl[rows, :]
        for cols in column_parts(0, (i + 1) * BLK):
            product = dot3(left_high, left_low, gh[now, :, cols], gl[now, :, cols])
            new = 2.0 * whole[0, rows, cols] - product
            whole[0, rows, cols] = new
        span = pl.ds(0, (i + 1) * BLK)
        yh[rows, span], yl[rows, span] = split(whole[0, rows, span])
        for j in range(i):
            other = pl.ds(j * BLK, BLK)
            turned = whole[0, rows, other].T
            whole[0, other, rows] = turned
            yh[other, rows], yl[other, rows] = split(turned)


def kernel(planes, t_hbm, p_hbm, noise_ref, mask_ref, read_ref, mean_ref, out_ref,
           mats, whole, gh, gl, yh, yl, offset, other_offset, xin, xmid, xout, xcur, ybase, bound,
           load_sem, send_sem, recv_sem, ready_sem):
    tm = lax.axis_index("tm")
    state = lax.axis_index("state")
    z, core = lax.div(tm, 2), lax.rem(tm, 2)
    products = sum((z >= first).astype(jnp.int32) for first in PRODUCT_FROM)
    late = products == SQUARINGS
    top = jnp.where(tm == 0, FIRST_TOPS[0], jnp.where(tm == 1, FIRST_TOPS[1], SQUARINGS))
    series = jnp.where(tm == 0, 2 ** (SQUARINGS + 1 - FIRST_TOPS[0]) - 1,
                       jnp.where(tm == 1, 2 ** (SQUARINGS + 1 - FIRST_TOPS[1]) - 1, 1))
    series = jnp.where(late, 0, series)
    has_gain = z >= GAIN_FROM
    has_map = z >= MAP_FROM
    ships = z >= SHIP_FROM
    entry_core = ships.astype(jnp.int32)
    next_entry = (z + 1 >= SHIP_FROM).astype(jnp.int32)
    has_next = jnp.logical_and(core == 1, z < planes - 1)
    has_before = jnp.logical_and(core == entry_core, z > 0)

    barrier = pltpu.get_barrier_semaphore()

    def greet(where):
        pl.semaphore_signal(barrier, inc=1, device_id=(where, state), device_id_type=MESH_ID)

    partner = z * 2 + 1 - core
    following = (z + 1) * 2 + next_entry
    greet(partner)

    @pl.when(has_next)
    def _():
        greet(following)

    @pl.when(has_before)
    def _():
        greet((z - 1) * 2 + 1)

    def band(i):
        return pl.ds(pl.multiple_of(i * LANE, LANE), LANE)

    def load_p(i):
        return pltpu.make_async_copy(p_hbm.at[band(i), :], mats.at[P_SLOT, band(i), :], load_sem.at[i])

    def start_load(i, carry):
        load_p(i).start()
        return carry

    bands = S // LANE
    lax.fori_loop(0, bands, start_load, 0)
    load_t = pltpu.make_async_copy(t_hbm, mats.at[T_SLOT], load_sem.at[bands])

    present = mask_ref[...].astype(f32)
    observed = present * read_ref[...]
    row_id = lax.broadcasted_iota(jnp.int32, (LANE, LANE), 0)
    col_id = lax.broadcasted_iota(jnp.int32, (LANE, LANE), 1)
    on_diagonal = row_id == col_id

    def present_down(i):
        down = jnp.broadcast_to(mask_ref[:, band(i)].astype(f32), (LANE, LANE)).T
        return jnp.concatenate([down] * bands, axis=1)

    def add_bands(pair, sums):
        for i in (2 * pair, 2 * pair + 1):
            load_p(i).wait()
        for i in (2 * pair, 2 * pair + 1):
            tile = jnp.abs(mats[P_SLOT, band(i), :]) * present_down(i)
            sums = sums + jnp.sum(tile.reshape(LANE // 8, 8, S), axis=0)
        return sums

    column_sums = jnp.sum(lax.fori_loop(0, bands // 2, add_bands, jnp.zeros((8, S), f32)), axis=0, keepdims=True)
    load_t.start()
    row_sums = present * column_sums + noise_ref[...]
    inverse_bound = 1.0 / jnp.max(row_sums, axis=1, keepdims=True)
    bound[...] = jnp.broadcast_to(inverse_bound, (1, LANE))

    def scale_bands(pair, carry):
        for i in (2 * pair, 2 * pair + 1):
            rows = band(i)
            across = present * bound[:, :1]
            tile = mats[P_SLOT, rows, :] * across * present_down(i)
            mats[0, rows, :] = tile
            gh[0, rows, :], gl[0, rows, :] = split(tile)
        for i in (2 * pair, 2 * pair + 1):
            rows = band(i)
            tile = mats[0, rows, rows] + jnp.where(on_diagonal, noise_ref[:, rows] * bound[...], 0.0)
            mats[0, rows, rows] = tile
            gh[0, rows, rows], gl[0, rows, rows] = split(tile)
        return carry

    lax.fori_loop(0, bands // 2, scale_bands, 0)

    @pl.when(products > 0)
    def _():
        def first_band(i, carry):
            rows = band(i)
            whole[0, rows, :] = mats[0, rows, :] * -bound[:, :1]
            tile = whole[0, rows, rows] + jnp.where(on_diagonal, 2.0 * bound[...], 0.0)
            whole[0, rows, rows] = tile
            yh[rows, :], yl[rows, :] = split(whole[0, rows, :])
            return carry

        lax.fori_loop(0, bands, first_band, 0)

    def two_squarings(pair, carry):
        @pl.when(jnp.logical_and(late, pair > 0))
        def _():
            multiply(whole, yh, yl, gh, gl, 0)

        @pl.when(2 * pair < top)
        def _():
            square(mats, 2 * pair, 2 * pair + 1, gh, gl, 0)

        @pl.when(late)
        def _():
            multiply(whole, yh, yl, gh, gl, 1)

        @pl.when(2 * pair + 1 < top)
        def _():
            square(mats, 2 * pair + 1, 2 * pair + 2, gh, gl, 1)

        return carry

    lax.fori_loop(0, lax.div(top + 1, 2), two_squarings, 0)

    def one_product(q, carry):
        def halve(i, inside):
            gh[0, band(i), :], gl[0, band(i), :] = split(mats[q, band(i), :])
            return inside

        lax.fori_loop(0, bands, halve, 0)
        multiply(whole, yh, yl, gh, gl, 0)
        return carry

    lax.fori_loop(1, jnp.where(late, 1, products + 1), one_product, 0)

    load_t.wait()

    pl.semaphore_wait(barrier, 1 + has_next.astype(jnp.int32) + has_before.astype(jnp.int32))

    def send(source, target, index, where):
        return pltpu.make_async_remote_copy(
            src_ref=source, dst_ref=target, send_sem=send_sem.at[index], recv_sem=recv_sem.at[index],
            device_id=(where, state), device_id_type=MESH_ID)

    mean_in = send(xout, xin, 0, following)
    map_over = send(mats.at[M_SLOT], mats.at[OTHER_SLOT], 1, partner)
    offset_over = send(offset, other_offset, 2, partner)
    hands = jnp.logical_and(ships, core == 0)
    takes = jnp.logical_and(ships, core == 1)

    @pl.when(takes)
    def _():
        pl.semaphore_signal(ready_sem, inc=1, device_id=(partner, state), device_id_type=MESH_ID)

    @pl.when(hands)
    def _():
        pl.semaphore_wait(ready_sem, 1)

    def block(i):
        return pl.ds(pl.multiple_of(i * BLK, BLK), BLK)

    @pl.when(has_gain)
    def _():
        def gain_rows(i, carry):
            rows = block(i)
            left_high, left_low = split(mats[P_SLOT, rows, :] * present)
            for cols in column_parts(0, S):
                mats[W_SLOT, rows, cols] = dot3(left_high, left_low, yh[:, cols], yl[:, cols])
            gh[1, rows, :], gl[1, rows, :] = split(mats[W_SLOT, rows, :] * present)
            gh[0, rows, :], gl[0, rows, :] = split(mats[T_SLOT, rows, :])
            return carry

        lax.fori_loop(0, S // BLK, gain_rows, 0)

    @pl.when(has_map)
    def _():
        offset[...] = matvec(mats, W_SLOT, observed)

        @pl.when(hands)
        def _():
            offset_over.start()

        def map_rows(i, carry):
            rows = block(i)
            for cols in column_parts(0, S):
                mats[M_SLOT, rows, cols] = mats[T_SLOT, rows, cols] - dot3(
                    gh[1, rows, :], gl[1, rows, :], gh[0, :, cols], gl[0, :, cols])

            @pl.when(hands)
            def _():
                send(mats.at[M_SLOT, rows, :], mats.at[OTHER_SLOT, rows, :], 1, partner).start()

            return carry

        lax.fori_loop(0, S // BLK, map_rows, 0)

    @pl.when(takes)
    def _():
        map_over.wait_recv()
        offset_over.wait_recv()

    middle_out = send(xmid, xin, 0, partner)
    inner_out = send(xout, xin, 0, partner)
    inner = jnp.logical_and(jnp.logical_not(ships), core == 0)
    low = jnp.where(products == 0, 0, products + 1)

    @pl.when(tm == 0)
    def _():
        xin[...] = mean_ref[...]

    @pl.when(tm > 0)
    def _():
        mean_in.wait_recv()

    @pl.when(jnp.logical_not(has_gain))
    def _():
        moved = matvec(mats, T_SLOT, xin[...])
        gap = observed - present * moved

        @pl.when(products == 0)
        def _():
            xcur[...] = gap * bound[:, :1]

        @pl.when(products > 0)
        def _():
            xcur[...] = matvec(whole, 0, gap)

        factors = jnp.maximum(top - low, 0)

        def apply(j, y):
            return 2.0 * y - matvec(mats, j, y)

        @pl.when(lax.rem(factors, 2) == 1)
        def _():
            xcur[...] = apply(low, xcur[...])

        def apply_two(pair, carry):
            j = top - 2 - 2 * pair
            xcur[...] = apply(j, apply(j + 1, xcur[...]))
            return carry

        lax.fori_loop(0, lax.div(factors, 2), apply_two, 0)
        ybase[...] = xcur[...]

        def add_power(y):
            return ybase[...] + (y - matvec(mats, top, y))

        @pl.when(series > 0)
        def _():
            xcur[...] = add_power(xcur[...])

        def add_two(step, carry):
            xcur[...] = add_power(add_power(xcur[...]))
            return carry

        lax.fori_loop(0, lax.div(series, 2), add_two, 0)
        xout[...] = moved + matvec(mats, P_SLOT, present * xcur[...])

    @pl.when(jnp.logical_and(has_gain, jnp.logical_not(has_map)))
    def _():
        moved = matvec(mats, T_SLOT, xin[...])
        xout[...] = moved + matvec(mats, W_SLOT, observed - present * moved)

    @pl.when(jnp.logical_and(has_map, jnp.logical_not(ships)))
    def _():
        xout[...] = matvec(mats, M_SLOT, xin[...]) + offset[...]

    @pl.when(takes)
    def _():
        middle = matvec(mats, OTHER_SLOT, xin[...]) + other_offset[...]
        xmid[...] = middle
        xout[...] = matvec(mats, M_SLOT, middle) + offset[...]

        @pl.when(has_next)
        def _():
            mean_in.start()

        middle_out.start()

    @pl.when(inner)
    def _():
        inner_out.start()

    @pl.when(jnp.logical_and(has_next, jnp.logical_not(ships)))
    def _():
        mean_in.start()

    @pl.when(hands)
    def _():
        xout[...] = xin[...]

    out_ref[...] = xout[...]

    @pl.when(inner)
    def _():
        inner_out.wait_send()

    @pl.when(has_next)
    def _():
        mean_in.wait_send()

    @pl.when(hands)
    def _():
        map_over.wait_send()
        offset_over.wait_send()

    @pl.when(takes)
    def _():
        middle_out.wait_send()


def per_device(transition, prior_cov, noise_var, sensor_mask, readings, prior_mean):
    planes = lax.axis_size("tm") // 2
    row = lambda value: value.reshape(1, S)
    vmem = pl.BlockSpec(memory_space=pltpu.VMEM)
    hbm = pl.BlockSpec(memory_space=pl.ANY)
    vector = pltpu.VMEM((1, S), f32)
    half, halves = pltpu.VMEM((S, S), bf16), pltpu.VMEM((2, S, S), bf16)
    mean = pl.pallas_call(
        functools.partial(kernel, planes),
        out_shape=jax.ShapeDtypeStruct((1, S), f32),
        in_specs=[hbm, hbm, vmem, vmem, vmem, vmem],
        out_specs=vmem,
        scratch_shapes=[
            pltpu.VMEM((10, S, S), f32), pltpu.VMEM((1, S, S), f32), halves, halves, half, half,
            *[vector] * 7, pltpu.VMEM((1, LANE), f32),
            pltpu.SemaphoreType.DMA((S // LANE + 1,)), pltpu.SemaphoreType.DMA((3,)), pltpu.SemaphoreType.DMA((3,)),
            pltpu.SemaphoreType.REGULAR,
        ],
        compiler_params=pltpu.CompilerParams(
            collective_id=0, has_side_effects=True, vmem_limit_bytes=63 * 2 ** 20),
    )(transition, prior_cov, row(noise_var), sensor_mask, readings, row(prior_mean))
    share = S // lax.axis_size("state")
    return lax.dynamic_slice_in_dim(mean, lax.axis_index("state") * share, share, 1)


def solution(mesh):
    placed = (P(), P(), P(), P("tm", None), P("tm", None), P())
    return jax.shard_map(
        per_device, mesh=mesh, in_specs=placed, out_specs=P("tm", "state"), check_vma=False
    )
```

```python
import functools
import jax
import jax.numpy as jnp
from jax import lax
from jax.experimental import pallas as pl
from jax.experimental.pallas import tpu as pltpu
from jax.sharding import PartitionSpec as P

f32 = jnp.float32
bf16 = jnp.bfloat16
S = 1024
BLK = 256
LANE = 128
WIDE = 512
SQUARINGS = 7
FIRST_TOPS = (4, 6)
T_SLOT, P_SLOT = 8, 9
W_SLOT, M_SLOT, OTHER_SLOT = 0, 1, 7

PRODUCT_FROM = (2, 2, 3, 3, 4, 5, 5)
GAIN_FROM = 7
MAP_FROM = 10
SHIP_FROM = 7
MESH_ID = pl.DeviceIdType.MESH


def split(value):
    high = value.astype(bf16)
    return high, (value - high.astype(f32)).astype(bf16)


def dot(left, right):
    return jnp.dot(left, right, preferred_element_type=f32)


def dot3(left_high, left_low, right_high, right_low):
    return dot(left_high, right_high) + dot(left_high, right_low) + dot(left_low, right_high)


def matvec(mats, slot, x):
    parts = []
    for i in range(S // LANE):
        total = None
        for k in range(S // LANE):
            tile = mats[slot, pl.ds(i * LANE, LANE), pl.ds(k * LANE, LANE)]
            term = tile * x[:, k * LANE:(k + 1) * LANE]
            total = term if total is None else total + term
        parts.append(jnp.sum(total.T, axis=0, keepdims=True))
    return jnp.concatenate(parts, axis=1)


def column_parts(start, stop):
    return [pl.ds(at, min(WIDE, stop - at)) for at in range(start, stop, WIDE)]


def square(mats, source, target, gh, gl, now):
    later = 1 - now
    for i in range(S // BLK):
        rows = pl.ds(i * BLK, BLK)
        left = gh[now, rows, :]
        for j in range(i + 1, S // BLK):
            cols = pl.ds(j * BLK, BLK)
            mats[target, cols, rows] = dot(left, gl[now, :, cols]).T
        for cols in column_parts(0, i * BLK):
            product = dot(left, gh[now, :, cols]) + dot(left, gl[now, :, cols])
            new = 2.0 * mats[source, rows, cols] - product - mats[target, rows, cols]
            mats[target, rows, cols] = new
            gh[later, rows, cols], gl[later, rows, cols] = split(new)
        cross = dot(left, gl[now, :, rows])
        new = 2.0 * mats[source, rows, rows] - dot(left, gh[now, :, rows]) - (cross + cross.T)
        mats[target, rows, rows] = new
        gh[later, rows, rows], gl[later, rows, rows] = split(new)
        for j in range(i):
            cols = pl.ds(j * BLK, BLK)
            turned = mats[target, rows, cols].T
            mats[target, cols, rows] = turned
            gh[later, cols, rows], gl[later, cols, rows] = split(turned)


def multiply(whole, yh, yl, gh, gl, now):
    for i in range(S // BLK):
        rows = pl.ds(i * BLK, BLK)
        left_high, left_low = yh[rows, :], yl[rows, :]
        for cols in column_parts(0, (i + 1) * BLK):
            product = dot3(left_high, left_low, gh[now, :, cols], gl[now, :, cols])
            new = 2.0 * whole[0, rows, cols] - product
            whole[0, rows, cols] = new
        span = pl.ds(0, (i + 1) * BLK)
        yh[rows, span], yl[rows, span] = split(whole[0, rows, span])
        for j in range(i):
            other = pl.ds(j * BLK, BLK)
            turned = whole[0, rows, other].T
            whole[0, other, rows] = turned
            yh[other, rows], yl[other, rows] = split(turned)


def kernel(planes, t_hbm, p_hbm, noise_ref, mask_ref, read_ref, mean_ref, out_ref,
           mats, whole, gh, gl, yh, yl, offset, other_offset, seen, other_seen, xin, xmid, xout, xcur, ybase, bound,
           load_sem, send_sem, recv_sem, ready_sem):
    tm = lax.axis_index("tm")
    state = lax.axis_index("state")
    z, core = lax.div(tm, 2), lax.rem(tm, 2)
    products = sum((z >= first).astype(jnp.int32) for first in PRODUCT_FROM)
    late = products == SQUARINGS
    top = jnp.where(tm == 0, FIRST_TOPS[0], jnp.where(tm == 1, FIRST_TOPS[1], SQUARINGS))
    series = jnp.where(tm == 0, 2 ** (SQUARINGS + 1 - FIRST_TOPS[0]) - 1,
                       jnp.where(tm == 1, 2 ** (SQUARINGS + 1 - FIRST_TOPS[1]) - 1, 1))
    series = jnp.where(late, 0, series)
    has_gain = z >= GAIN_FROM
    has_map = z >= MAP_FROM
    ships = z >= SHIP_FROM
    entry_core = ships.astype(jnp.int32)
    next_entry = (z + 1 >= SHIP_FROM).astype(jnp.int32)
    has_next = jnp.logical_and(core == 1, z < planes - 1)
    has_before = jnp.logical_and(core == entry_core, z > 0)

    barrier = pltpu.get_barrier_semaphore()

    def greet(where):
        pl.semaphore_signal(barrier, inc=1, device_id=(where, state), device_id_type=MESH_ID)

    partner = z * 2 + 1 - core
    following = (z + 1) * 2 + next_entry
    greet(partner)

    @pl.when(has_next)
    def _():
        greet(following)

    @pl.when(has_before)
    def _():
        greet((z - 1) * 2 + 1)

    def band(i):
        return pl.ds(pl.multiple_of(i * LANE, LANE), LANE)

    def load_p(i):
        return pltpu.make_async_copy(p_hbm.at[band(i), :], mats.at[P_SLOT, band(i), :], load_sem.at[i])

    def start_load(i, carry):
        load_p(i).start()
        return carry

    bands = S // LANE
    lax.fori_loop(0, bands, start_load, 0)
    load_t = pltpu.make_async_copy(t_hbm, mats.at[T_SLOT], load_sem.at[bands])

    present = mask_ref[...].astype(f32)
    observed = present * read_ref[...]
    row_id = lax.broadcasted_iota(jnp.int32, (LANE, LANE), 0)
    col_id = lax.broadcasted_iota(jnp.int32, (LANE, LANE), 1)
    on_diagonal = row_id == col_id

    def present_down(i):
        down = jnp.broadcast_to(mask_ref[:, band(i)].astype(f32), (LANE, LANE)).T
        return jnp.concatenate([down] * bands, axis=1)

    def add_bands(pair, sums):
        for i in (2 * pair, 2 * pair + 1):
            load_p(i).wait()
        for i in (2 * pair, 2 * pair + 1):
            tile = jnp.abs(mats[P_SLOT, band(i), :]) * present_down(i)
            sums = sums + jnp.sum(tile.reshape(LANE // 8, 8, S), axis=0)
        return sums

    column_sums = jnp.sum(lax.fori_loop(0, bands // 2, add_bands, jnp.zeros((8, S), f32)), axis=0, keepdims=True)
    load_t.start()
    row_sums = present * column_sums + noise_ref[...]
    inverse_bound = 1.0 / jnp.max(row_sums, axis=1, keepdims=True)
    bound[...] = jnp.broadcast_to(inverse_bound, (1, LANE))

    def scale_bands(pair, carry):
        for i in (2 * pair, 2 * pair + 1):
            rows = band(i)
            across = present * bound[:, :1]
            tile = mats[P_SLOT, rows, :] * across * present_down(i)
            mats[0, rows, :] = tile
            gh[0, rows, :], gl[0, rows, :] = split(tile)
        for i in (2 * pair, 2 * pair + 1):
            rows = band(i)
            tile = mats[0, rows, rows] + jnp.where(on_diagonal, noise_ref[:, rows] * bound[...], 0.0)
            mats[0, rows, rows] = tile
            gh[0, rows, rows], gl[0, rows, rows] = split(tile)
        return carry

    lax.fori_loop(0, bands // 2, scale_bands, 0)

    @pl.when(products > 0)
    def _():
        def first_band(i, carry):
            rows = band(i)
            whole[0, rows, :] = mats[0, rows, :] * -bound[:, :1]
            tile = whole[0, rows, rows] + jnp.where(on_diagonal, 2.0 * bound[...], 0.0)
            whole[0, rows, rows] = tile
            yh[rows, :], yl[rows, :] = split(whole[0, rows, :])
            return carry

        lax.fori_loop(0, bands, first_band, 0)

    def two_squarings(pair, carry):
        first = 2 * pair

        @pl.when(jnp.logical_and(first > 0, first <= products))
        def _():
            multiply(whole, yh, yl, gh, gl, 0)

        @pl.when(first < top)
        def _():
            square(mats, first, first + 1, gh, gl, 0)

        @pl.when(first + 1 <= products)
        def _():
            multiply(whole, yh, yl, gh, gl, 1)

        @pl.when(first + 1 < top)
        def _():
            square(mats, first + 1, first + 2, gh, gl, 1)

        return carry

    lax.fori_loop(0, lax.div(top + 1, 2), two_squarings, 0)

    load_t.wait()

    pl.semaphore_wait(barrier, 1 + has_next.astype(jnp.int32) + has_before.astype(jnp.int32))

    def send(source, target, index, where):
        return pltpu.make_async_remote_copy(
            src_ref=source, dst_ref=target, send_sem=send_sem.at[index], recv_sem=recv_sem.at[index],
            device_id=(where, state), device_id_type=MESH_ID)

    mean_in = send(xout, xin, 0, following)
    matrix_over = send(mats.at[M_SLOT], mats.at[OTHER_SLOT], 1, partner)
    present_over = send(seen, other_seen, 3, partner)
    offset_over = send(offset, other_offset, 2, partner)
    hands = jnp.logical_and(ships, core == 0)
    takes = jnp.logical_and(ships, core == 1)

    @pl.when(takes)
    def _():
        pl.semaphore_signal(ready_sem, inc=1, device_id=(partner, state), device_id_type=MESH_ID)

    @pl.when(hands)
    def _():
        pl.semaphore_wait(ready_sem, 1)

    def block(i):
        return pl.ds(pl.multiple_of(i * BLK, BLK), BLK)

    offset[...] = observed
    seen[...] = present

    @pl.when(jnp.logical_and(hands, jnp.logical_not(has_map)))
    def _():
        offset_over.start()
        present_over.start()

    @pl.when(has_gain)
    def _():
        def gain_rows(i, carry):
            rows = block(i)
            left_high, left_low = split(mats[P_SLOT, rows, :] * present)
            for cols in column_parts(0, S):
                mats[W_SLOT, rows, cols] = dot3(left_high, left_low, yh[:, cols], yl[:, cols])

            @pl.when(jnp.logical_and(hands, jnp.logical_not(has_map)))
            def _():
                send(mats.at[W_SLOT, rows, :], mats.at[OTHER_SLOT, rows, :], 1, partner).start()

            gh[1, rows, :], gl[1, rows, :] = split(mats[W_SLOT, rows, :] * present)
            gh[0, rows, :], gl[0, rows, :] = split(mats[T_SLOT, rows, :])
            return carry

        lax.fori_loop(0, S // BLK, gain_rows, 0)

    @pl.when(has_map)
    def _():
        def map_rows(i, carry):
            rows = block(i)
            for cols in column_parts(0, S):
                mats[M_SLOT, rows, cols] = mats[T_SLOT, rows, cols] - dot3(
                    gh[1, rows, :], gl[1, rows, :], gh[0, :, cols], gl[0, :, cols])

            @pl.when(hands)
            def _():
                send(mats.at[M_SLOT, rows, :], mats.at[OTHER_SLOT, rows, :], 1, partner).start()

            return carry

        lax.fori_loop(0, S // BLK, map_rows, 0)
        offset[...] = matvec(mats, W_SLOT, observed)

        @pl.when(hands)
        def _():
            offset_over.start()

    @pl.when(takes)
    def _():
        matrix_over.wait_recv()
        offset_over.wait_recv()

    @pl.when(jnp.logical_and(takes, jnp.logical_not(has_map)))
    def _():
        present_over.wait_recv()

    middle_out = send(xmid, xin, 0, partner)
    inner_out = send(xout, xin, 0, partner)
    inner = jnp.logical_and(jnp.logical_not(ships), core == 0)
    low = jnp.where(products == 0, 0, products + 1)

    @pl.when(tm == 0)
    def _():
        xin[...] = mean_ref[...]

    @pl.when(tm > 0)
    def _():
        mean_in.wait_recv()

    @pl.when(jnp.logical_not(has_gain))
    def _():
        moved = matvec(mats, T_SLOT, xin[...])
        gap = observed - present * moved

        @pl.when(products == 0)
        def _():
            xcur[...] = gap * bound[:, :1]

        @pl.when(products > 0)
        def _():
            xcur[...] = matvec(whole, 0, gap)

        factors = jnp.maximum(top - low, 0)

        def apply(j, y):
            return 2.0 * y - matvec(mats, j, y)

        @pl.when(lax.rem(factors, 2) == 1)
        def _():
            xcur[...] = apply(low, xcur[...])

        def apply_two(pair, carry):
            j = top - 2 - 2 * pair
            xcur[...] = apply(j, apply(j + 1, xcur[...]))
            return carry

        lax.fori_loop(0, lax.div(factors, 2), apply_two, 0)
        ybase[...] = xcur[...]

        def add_power(y):
            return ybase[...] + (y - matvec(mats, top, y))

        @pl.when(series > 0)
        def _():
            xcur[...] = add_power(xcur[...])

        def add_two(step, carry):
            xcur[...] = add_power(add_power(xcur[...]))
            return carry

        lax.fori_loop(0, lax.div(series, 2), add_two, 0)
        xout[...] = moved + matvec(mats, P_SLOT, present * xcur[...])

    @pl.when(jnp.logical_and(has_gain, jnp.logical_not(jnp.logical_or(has_map, ships))))
    def _():
        moved = matvec(mats, T_SLOT, xin[...])
        xout[...] = moved + matvec(mats, W_SLOT, observed - present * moved)

    @pl.when(jnp.logical_and(has_map, jnp.logical_not(ships)))
    def _():
        xout[...] = matvec(mats, M_SLOT, xin[...]) + offset[...]

    @pl.when(jnp.logical_and(takes, jnp.logical_not(has_map)))
    def _():
        moved = matvec(mats, T_SLOT, xin[...])
        middle = moved + matvec(mats, OTHER_SLOT, other_offset[...] - other_seen[...] * moved)
        xmid[...] = middle
        moved = matvec(mats, T_SLOT, middle)
        xout[...] = moved + matvec(mats, W_SLOT, observed - present * moved)

        @pl.when(has_next)
        def _():
            mean_in.start()

        middle_out.start()

    @pl.when(jnp.logical_and(takes, has_map))
    def _():
        middle = matvec(mats, OTHER_SLOT, xin[...]) + other_offset[...]
        xmid[...] = middle
        xout[...] = matvec(mats, M_SLOT, middle) + offset[...]

        @pl.when(has_next)
        def _():
            mean_in.start()

        middle_out.start()

    @pl.when(inner)
    def _():
        inner_out.start()

    @pl.when(jnp.logical_and(has_next, jnp.logical_not(ships)))
    def _():
        mean_in.start()

    @pl.when(hands)
    def _():
        xout[...] = xin[...]

    out_ref[...] = xout[...]

    @pl.when(inner)
    def _():
        inner_out.wait_send()

    @pl.when(has_next)
    def _():
        mean_in.wait_send()

    @pl.when(hands)
    def _():
        matrix_over.wait_send()
        offset_over.wait_send()

    @pl.when(jnp.logical_and(hands, jnp.logical_not(has_map)))
    def _():
        present_over.wait_send()

    @pl.when(takes)
    def _():
        middle_out.wait_send()


def per_device(transition, prior_cov, noise_var, sensor_mask, readings, prior_mean):
    planes = lax.axis_size("tm") // 2
    row = lambda value: value.reshape(1, S)
    vmem = pl.BlockSpec(memory_space=pltpu.VMEM)
    hbm = pl.BlockSpec(memory_space=pl.ANY)
    vector = pltpu.VMEM((1, S), f32)
    half, halves = pltpu.VMEM((S, S), bf16), pltpu.VMEM((2, S, S), bf16)
    mean = pl.pallas_call(
        functools.partial(kernel, planes),
        out_shape=jax.ShapeDtypeStruct((1, S), f32),
        in_specs=[hbm, hbm, vmem, vmem, vmem, vmem],
        out_specs=vmem,
        scratch_shapes=[
            pltpu.VMEM((10, S, S), f32), pltpu.VMEM((1, S, S), f32), halves, halves, half, half,
            *[vector] * 9, pltpu.VMEM((1, LANE), f32),
            pltpu.SemaphoreType.DMA((S // LANE + 1,)), pltpu.SemaphoreType.DMA((4,)), pltpu.SemaphoreType.DMA((4,)),
            pltpu.SemaphoreType.REGULAR,
        ],
        compiler_params=pltpu.CompilerParams(
            collective_id=0, has_side_effects=True, vmem_limit_bytes=63 * 2 ** 20),
    )(transition, prior_cov, row(noise_var), sensor_mask, readings, row(prior_mean))
    share = S // lax.axis_size("state")
    return lax.dynamic_slice_in_dim(mean, lax.axis_index("state") * share, share, 1)


def solution(mesh):
    placed = (P(), P(), P(), P("tm", None), P("tm", None), P())
    return jax.shard_map(
        per_device, mesh=mesh, in_specs=placed, out_specs=P("tm", "state"), check_vma=False
    )
```

```python
import functools
import jax
import jax.numpy as jnp
from jax import lax
from jax.experimental import pallas as pl
from jax.experimental.pallas import tpu as pltpu
from jax.sharding import PartitionSpec as P

f32 = jnp.float32
bf16 = jnp.bfloat16
S = 1024
BLK = 256
LANE = 128
WIDE = 512
SQUARINGS = 7
FIRST_TOPS = (4, 6)
T_SLOT, P_SLOT = 8, 9
W_SLOT, M_SLOT, OTHER_SLOT = 0, 1, 7

PRODUCT_FROM = (2, 2, 3, 3, 4, 5, 5)
GAIN_FROM = 7
MAP_FROM = 10
SHIP_FROM = 7
JOIN_FROM = 12
MESH_ID = pl.DeviceIdType.MESH


def split(value):
    high = value.astype(bf16)
    return high, (value - high.astype(f32)).astype(bf16)


def dot(left, right):
    return jnp.dot(left, right, preferred_element_type=f32)


def dot3(left_high, left_low, right_high, right_low):
    return dot(left_high, right_high) + dot(left_high, right_low) + dot(left_low, right_high)


def matvec(mats, slot, x):
    parts = []
    for i in range(S // LANE):
        total = None
        for k in range(S // LANE):
            tile = mats[slot, pl.ds(i * LANE, LANE), pl.ds(k * LANE, LANE)]
            term = tile * x[:, k * LANE:(k + 1) * LANE]
            total = term if total is None else total + term
        parts.append(jnp.sum(total.T, axis=0, keepdims=True))
    return jnp.concatenate(parts, axis=1)


def column_parts(start, stop):
    return [pl.ds(at, min(WIDE, stop - at)) for at in range(start, stop, WIDE)]


def square(mats, source, target, gh, gl, now):
    later = 1 - now
    for i in range(S // BLK):
        rows = pl.ds(i * BLK, BLK)
        left = gh[now, rows, :]
        for j in range(i + 1, S // BLK):
            cols = pl.ds(j * BLK, BLK)
            mats[target, cols, rows] = dot(left, gl[now, :, cols]).T
        for cols in column_parts(0, i * BLK):
            product = dot(left, gh[now, :, cols]) + dot(left, gl[now, :, cols])
            new = 2.0 * mats[source, rows, cols] - product - mats[target, rows, cols]
            mats[target, rows, cols] = new
            gh[later, rows, cols], gl[later, rows, cols] = split(new)
        cross = dot(left, gl[now, :, rows])
        new = 2.0 * mats[source, rows, rows] - dot(left, gh[now, :, rows]) - (cross + cross.T)
        mats[target, rows, rows] = new
        gh[later, rows, rows], gl[later, rows, rows] = split(new)
        for j in range(i):
            cols = pl.ds(j * BLK, BLK)
            turned = mats[target, rows, cols].T
            mats[target, cols, rows] = turned
            gh[later, cols, rows], gl[later, cols, rows] = split(turned)


def multiply(whole, yh, yl, gh, gl, now):
    for i in range(S // BLK):
        rows = pl.ds(i * BLK, BLK)
        left_high, left_low = yh[rows, :], yl[rows, :]
        for cols in column_parts(0, (i + 1) * BLK):
            product = dot3(left_high, left_low, gh[now, :, cols], gl[now, :, cols])
            new = 2.0 * whole[0, rows, cols] - product
            whole[0, rows, cols] = new
        span = pl.ds(0, (i + 1) * BLK)
        yh[rows, span], yl[rows, span] = split(whole[0, rows, span])
        for j in range(i):
            other = pl.ds(j * BLK, BLK)
            turned = whole[0, rows, other].T
            whole[0, other, rows] = turned
            yh[other, rows], yl[other, rows] = split(turned)


def kernel(planes, t_hbm, p_hbm, noise_ref, mask_ref, read_ref, mean_ref, out_ref,
           mats, whole, gh, gl, yh, yl, offset, other_offset, seen, other_seen, xin, xmid, xout, xcur, ybase, bound,
           load_sem, send_sem, recv_sem, ready_sem):
    tm = lax.axis_index("tm")
    state = lax.axis_index("state")
    z, core = lax.div(tm, 2), lax.rem(tm, 2)
    products = sum((z >= first).astype(jnp.int32) for first in PRODUCT_FROM)
    late = products == SQUARINGS
    top = jnp.where(tm == 0, FIRST_TOPS[0], jnp.where(tm == 1, FIRST_TOPS[1], SQUARINGS))
    series = jnp.where(tm == 0, 2 ** (SQUARINGS + 1 - FIRST_TOPS[0]) - 1,
                       jnp.where(tm == 1, 2 ** (SQUARINGS + 1 - FIRST_TOPS[1]) - 1, 1))
    series = jnp.where(late, 0, series)
    has_gain = z >= GAIN_FROM
    has_map = z >= MAP_FROM
    ships = z >= SHIP_FROM
    joins = jnp.logical_and(jnp.logical_and(core == 1, z >= JOIN_FROM), z < planes - 1)
    entry_core = ships.astype(jnp.int32)
    next_entry = (z + 1 >= SHIP_FROM).astype(jnp.int32)
    has_next = jnp.logical_and(core == 1, z < planes - 1)
    has_before = jnp.logical_and(core == entry_core, z > 0)

    barrier = pltpu.get_barrier_semaphore()

    def greet(where):
        pl.semaphore_signal(barrier, inc=1, device_id=(where, state), device_id_type=MESH_ID)

    partner = z * 2 + 1 - core
    following = (z + 1) * 2 + next_entry
    greet(partner)

    @pl.when(has_next)
    def _():
        greet(following)

    @pl.when(has_before)
    def _():
        greet((z - 1) * 2 + 1)

    def band(i):
        return pl.ds(pl.multiple_of(i * LANE, LANE), LANE)

    def load_p(i):
        return pltpu.make_async_copy(p_hbm.at[band(i), :], mats.at[P_SLOT, band(i), :], load_sem.at[i])

    def start_load(i, carry):
        load_p(i).start()
        return carry

    bands = S // LANE
    lax.fori_loop(0, bands, start_load, 0)
    load_t = pltpu.make_async_copy(t_hbm, mats.at[T_SLOT], load_sem.at[bands])

    present = mask_ref[...].astype(f32)
    observed = present * read_ref[...]
    row_id = lax.broadcasted_iota(jnp.int32, (LANE, LANE), 0)
    col_id = lax.broadcasted_iota(jnp.int32, (LANE, LANE), 1)
    on_diagonal = row_id == col_id

    def present_down(i):
        down = jnp.broadcast_to(mask_ref[:, band(i)].astype(f32), (LANE, LANE)).T
        return jnp.concatenate([down] * bands, axis=1)

    def add_bands(pair, sums):
        for i in (2 * pair, 2 * pair + 1):
            load_p(i).wait()
        for i in (2 * pair, 2 * pair + 1):
            tile = jnp.abs(mats[P_SLOT, band(i), :]) * present_down(i)
            sums = sums + jnp.sum(tile.reshape(LANE // 8, 8, S), axis=0)
        return sums

    column_sums = jnp.sum(lax.fori_loop(0, bands // 2, add_bands, jnp.zeros((8, S), f32)), axis=0, keepdims=True)
    load_t.start()
    row_sums = present * column_sums + noise_ref[...]
    inverse_bound = 1.0 / jnp.max(row_sums, axis=1, keepdims=True)
    bound[...] = jnp.broadcast_to(inverse_bound, (1, LANE))

    def scale_bands(pair, carry):
        for i in (2 * pair, 2 * pair + 1):
            rows = band(i)
            across = present * bound[:, :1]
            tile = mats[P_SLOT, rows, :] * across * present_down(i)
            mats[0, rows, :] = tile
            gh[0, rows, :], gl[0, rows, :] = split(tile)
        for i in (2 * pair, 2 * pair + 1):
            rows = band(i)
            tile = mats[0, rows, rows] + jnp.where(on_diagonal, noise_ref[:, rows] * bound[...], 0.0)
            mats[0, rows, rows] = tile
            gh[0, rows, rows], gl[0, rows, rows] = split(tile)
        return carry

    lax.fori_loop(0, bands // 2, scale_bands, 0)

    @pl.when(products > 0)
    def _():
        def first_band(i, carry):
            rows = band(i)
            whole[0, rows, :] = mats[0, rows, :] * -bound[:, :1]
            tile = whole[0, rows, rows] + jnp.where(on_diagonal, 2.0 * bound[...], 0.0)
            whole[0, rows, rows] = tile
            yh[rows, :], yl[rows, :] = split(whole[0, rows, :])
            return carry

        lax.fori_loop(0, bands, first_band, 0)

    def two_squarings(pair, carry):
        first = 2 * pair

        @pl.when(jnp.logical_and(first > 0, first <= products))
        def _():
            multiply(whole, yh, yl, gh, gl, 0)

        @pl.when(first < top)
        def _():
            square(mats, first, first + 1, gh, gl, 0)

        @pl.when(first + 1 <= products)
        def _():
            multiply(whole, yh, yl, gh, gl, 1)

        @pl.when(first + 1 < top)
        def _():
            square(mats, first + 1, first + 2, gh, gl, 1)

        return carry

    lax.fori_loop(0, lax.div(top + 1, 2), two_squarings, 0)

    load_t.wait()

    pl.semaphore_wait(barrier, 1 + has_next.astype(jnp.int32) + has_before.astype(jnp.int32))

    def send(source, target, index, where):
        return pltpu.make_async_remote_copy(
            src_ref=source, dst_ref=target, send_sem=send_sem.at[index], recv_sem=recv_sem.at[index],
            device_id=(where, state), device_id_type=MESH_ID)

    mean_in = send(xout, xin, 0, following)
    matrix_over = send(mats.at[M_SLOT], mats.at[OTHER_SLOT], 1, partner)
    present_over = send(seen, other_seen, 3, partner)
    offset_over = send(offset, other_offset, 2, partner)
    hands = jnp.logical_and(ships, core == 0)
    takes = jnp.logical_and(ships, core == 1)

    @pl.when(takes)
    def _():
        pl.semaphore_signal(ready_sem, inc=1, device_id=(partner, state), device_id_type=MESH_ID)

    @pl.when(hands)
    def _():
        pl.semaphore_wait(ready_sem, 1)

    def block(i):
        return pl.ds(pl.multiple_of(i * BLK, BLK), BLK)

    offset[...] = observed
    seen[...] = present

    @pl.when(jnp.logical_and(hands, jnp.logical_not(has_map)))
    def _():
        offset_over.start()
        present_over.start()

    @pl.when(has_gain)
    def _():
        def gain_rows(i, carry):
            rows = block(i)
            left_high, left_low = split(mats[P_SLOT, rows, :] * present)
            for cols in column_parts(0, S):
                mats[W_SLOT, rows, cols] = dot3(left_high, left_low, yh[:, cols], yl[:, cols])

            @pl.when(jnp.logical_and(hands, jnp.logical_not(has_map)))
            def _():
                send(mats.at[W_SLOT, rows, :], mats.at[OTHER_SLOT, rows, :], 1, partner).start()

            gh[1, rows, :], gl[1, rows, :] = split(mats[W_SLOT, rows, :] * present)
            gh[0, rows, :], gl[0, rows, :] = split(mats[T_SLOT, rows, :])
            return carry

        lax.fori_loop(0, S // BLK, gain_rows, 0)

    @pl.when(has_map)
    def _():
        def map_rows(i, carry):
            rows = block(i)
            for cols in column_parts(0, S):
                mats[M_SLOT, rows, cols] = mats[T_SLOT, rows, cols] - dot3(
                    gh[1, rows, :], gl[1, rows, :], gh[0, :, cols], gl[0, :, cols])

            @pl.when(hands)
            def _():
                send(mats.at[M_SLOT, rows, :], mats.at[OTHER_SLOT, rows, :], 1, partner).start()

            return carry

        lax.fori_loop(0, S // BLK, map_rows, 0)
        offset[...] = matvec(mats, W_SLOT, observed)

        @pl.when(hands)
        def _():
            offset_over.start()

    @pl.when(takes)
    def _():
        matrix_over.wait_recv()
        offset_over.wait_recv()

    @pl.when(jnp.logical_and(takes, jnp.logical_not(has_map)))
    def _():
        present_over.wait_recv()

    @pl.when(joins)
    def _():
        def halve_other(i, carry):
            yh[band(i), :], yl[band(i), :] = split(mats[OTHER_SLOT, band(i), :])
            return carry

        lax.fori_loop(0, bands, halve_other, 0)

        def join_rows(i, carry):
            rows = block(i)
            left_high, left_low = split(mats[M_SLOT, rows, :])
            for cols in column_parts(0, S):
                mats[W_SLOT, rows, cols] = dot3(left_high, left_low, yh[:, cols], yl[:, cols])
            return carry

        lax.fori_loop(0, S // BLK, join_rows, 0)
        seen[...] = matvec(mats, M_SLOT, other_offset[...]) + offset[...]

    middle_out = send(xmid, xin, 0, partner)
    inner_out = send(xout, xin, 0, partner)
    inner = jnp.logical_and(jnp.logical_not(ships), core == 0)
    low = jnp.where(products == 0, 0, products + 1)

    @pl.when(tm == 0)
    def _():
        xin[...] = mean_ref[...]

    @pl.when(tm > 0)
    def _():
        mean_in.wait_recv()

    @pl.when(jnp.logical_not(has_gain))
    def _():
        moved = matvec(mats, T_SLOT, xin[...])
        gap = observed - present * moved

        @pl.when(products == 0)
        def _():
            xcur[...] = gap * bound[:, :1]

        @pl.when(products > 0)
        def _():
            xcur[...] = matvec(whole, 0, gap)

        factors = jnp.maximum(top - low, 0)

        def apply(j, y):
            return 2.0 * y - matvec(mats, j, y)

        @pl.when(lax.rem(factors, 2) == 1)
        def _():
            xcur[...] = apply(low, xcur[...])

        def apply_two(pair, carry):
            j = top - 2 - 2 * pair
            xcur[...] = apply(j, apply(j + 1, xcur[...]))
            return carry

        lax.fori_loop(0, lax.div(factors, 2), apply_two, 0)
        ybase[...] = xcur[...]

        def add_power(y):
            return ybase[...] + (y - matvec(mats, top, y))

        @pl.when(series > 0)
        def _():
            xcur[...] = add_power(xcur[...])

        def add_two(step, carry):
            xcur[...] = add_power(add_power(xcur[...]))
            return carry

        lax.fori_loop(0, lax.div(series, 2), add_two, 0)
        xout[...] = moved + matvec(mats, P_SLOT, present * xcur[...])

    @pl.when(jnp.logical_and(has_gain, jnp.logical_not(jnp.logical_or(has_map, ships))))
    def _():
        moved = matvec(mats, T_SLOT, xin[...])
        xout[...] = moved + matvec(mats, W_SLOT, observed - present * moved)

    @pl.when(jnp.logical_and(has_map, jnp.logical_not(ships)))
    def _():
        xout[...] = matvec(mats, M_SLOT, xin[...]) + offset[...]

    @pl.when(jnp.logical_and(takes, jnp.logical_not(has_map)))
    def _():
        moved = matvec(mats, T_SLOT, xin[...])
        middle = moved + matvec(mats, OTHER_SLOT, other_offset[...] - other_seen[...] * moved)
        xmid[...] = middle
        moved = matvec(mats, T_SLOT, middle)
        xout[...] = moved + matvec(mats, W_SLOT, observed - present * moved)

        @pl.when(has_next)
        def _():
            mean_in.start()

        middle_out.start()

    @pl.when(jnp.logical_and(jnp.logical_and(takes, has_map), jnp.logical_not(joins)))
    def _():
        middle = matvec(mats, OTHER_SLOT, xin[...]) + other_offset[...]
        xmid[...] = middle

        @pl.when(jnp.logical_not(has_next))
        def _():
            middle_out.start()

        xout[...] = matvec(mats, M_SLOT, middle) + offset[...]

        @pl.when(has_next)
        def _():
            mean_in.start()
            middle_out.start()

    @pl.when(joins)
    def _():
        xout[...] = matvec(mats, W_SLOT, xin[...]) + seen[...]
        mean_in.start()
        xmid[...] = matvec(mats, OTHER_SLOT, xin[...]) + other_offset[...]
        middle_out.start()

    @pl.when(inner)
    def _():
        inner_out.start()

    @pl.when(jnp.logical_and(has_next, jnp.logical_not(ships)))
    def _():
        mean_in.start()

    @pl.when(hands)
    def _():
        xout[...] = xin[...]

    out_ref[...] = xout[...]

    @pl.when(inner)
    def _():
        inner_out.wait_send()

    @pl.when(has_next)
    def _():
        mean_in.wait_send()

    @pl.when(hands)
    def _():
        matrix_over.wait_send()
        offset_over.wait_send()

    @pl.when(jnp.logical_and(hands, jnp.logical_not(has_map)))
    def _():
        present_over.wait_send()

    @pl.when(takes)
    def _():
        middle_out.wait_send()


def per_device(transition, prior_cov, noise_var, sensor_mask, readings, prior_mean):
    planes = lax.axis_size("tm") // 2
    row = lambda value: value.reshape(1, S)
    vmem = pl.BlockSpec(memory_space=pltpu.VMEM)
    hbm = pl.BlockSpec(memory_space=pl.ANY)
    vector = pltpu.VMEM((1, S), f32)
    half, halves = pltpu.VMEM((S, S), bf16), pltpu.VMEM((2, S, S), bf16)
    mean = pl.pallas_call(
        functools.partial(kernel, planes),
        out_shape=jax.ShapeDtypeStruct((1, S), f32),
        in_specs=[hbm, hbm, vmem, vmem, vmem, vmem],
        out_specs=vmem,
        scratch_shapes=[
            pltpu.VMEM((10, S, S), f32), pltpu.VMEM((1, S, S), f32), halves, halves, half, half,
            *[vector] * 9, pltpu.VMEM((1, LANE), f32),
            pltpu.SemaphoreType.DMA((S // LANE + 1,)), pltpu.SemaphoreType.DMA((4,)), pltpu.SemaphoreType.DMA((4,)),
            pltpu.SemaphoreType.REGULAR,
        ],
        compiler_params=pltpu.CompilerParams(
            collective_id=0, has_side_effects=True, vmem_limit_bytes=63 * 2 ** 20),
    )(transition, prior_cov, row(noise_var), sensor_mask, readings, row(prior_mean))
    share = S // lax.axis_size("state")
    return lax.dynamic_slice_in_dim(mean, lax.axis_index("state") * share, share, 1)


def solution(mesh):
    placed = (P(), P(), P(), P("tm", None), P("tm", None), P())
    return jax.shard_map(
        per_device, mesh=mesh, in_specs=placed, out_specs=P("tm", "state"), check_vma=False
    )
```
